512 devices in a mesh: section: 4 (over z_hi), dp: 32 (over x, y), tensor: 4 (over z_lo, core).
Axes of the slice: x: 4, y: 8, z: 8 (z_hi: 4, z_lo: 2; z = z_hi * 2 + z_lo), core: 2. Of those that a mesh axis runs over, the one named last changes fastest.
Arguments:
- top_grad: bfloat16 [4, 2048, 8192], P(None, 'dp', 'tensor'), may hold values from -6 to 6
- stash: bfloat16 [4, 4, 2048, 8192], P('section', None, 'dp', 'tensor'), may hold values from -6 to 6
- value_grad: bfloat16 [4, 4, 2048, 512], P('section', None, 'dp', 'tensor'), may hold values from -6 to 6
- value_weight: bfloat16 [4, 512, 8192], P('section', 'dp', 'tensor'), may hold values from -0.25 to 0.25
- left_stats: float32 [4, 16, 512, 512], P('section', 'tensor', 'dp'), as said below
- right_stats: float32 [4, 16, 512, 512], P('section', 'tensor', 'dp'), as said below
- refresh: int32 [4, 4, 2], P('section', 'tensor'), may hold values from 0 to 3, as said below
- order: int32 [4], replicated, may hold values from 0 to 3, each once
Outputs:
- input_grad: bfloat16 [4, 4, 2048, 8192], P('section', None, 'dp', 'tensor')
- weight_grad: float32 [4, 512, 8192], P('section', 'dp', 'tensor')
- new_left: float32 [4, 16, 512, 512], P('section', 'tensor', 'dp')
- new_right: float32 [4, 16, 512, 512], P('section', 'tensor', 'dp')
- roots: float32 [4, 4, 4, 512, 512], P('section', 'tensor', None, 'dp')
The draws below stay inside these ranges and needn't reach their ends.
Inputs may be any that keep to these rules, and one draw needn't show every extreme that they name: `refresh`: each row holds 2 consecutive block numbers modulo 4, from a start drawn for each row. `order`: A permutation of the micro-batches. `left_stats`: each matrix is symmetric positive definite. `right_stats`: each matrix is symmetric positive definite.
All inputs are finite; a program needn't handle non-finite values.
Results may differ from the reference program's by a relative error of at most 0.015.
Values may be sent and summed in bfloat16 or wider, within the bound.
No kernel may reach another device: no remote copies, remote signals or barrier semaphores. Data moves between devices by JAX's collectives and lax.ppermute only.
A program may use at most 64 MiB of HBM per device.

```python
import jax
import jax.numpy as jnp
from jax import lax

D = 8192
KV = 512
TOK_DEV = 64
MICRO = 4
NREF = 2
ITERS = 2
SECTIONS = 4
GROUPS = 32
TENSORS = 4
TOKENS = 2048
BLOCKS = 16
BLK_T = 4


def stat_matrix(key, exponent, corr, strength):
    key_rank, key_diag = jax.random.split(key)
    rank_keys = jax.random.split(key_rank, SECTIONS * BLOCKS)
    ranks = jax.vmap(lambda one_key: jax.random.permutation(one_key, KV))(rank_keys)
    ranks = ranks.reshape(SECTIONS, BLOCKS, KV).astype(jnp.float32)
    weights = jnp.power(ranks + 1.0, -exponent) * (strength * KV * MICRO * TOKENS)
    jitter = jax.random.uniform(key_diag, (SECTIONS, BLOCKS, KV), jnp.float32, 0.1, 0.5)
    position = jnp.arange(KV, dtype=jnp.float32)
    distance = jnp.abs(position[:, None] - position[None, :])
    identity = jnp.eye(KV, dtype=jnp.float32)
    kernel = jnp.power(corr, distance)[None, None] + jitter[..., None] * identity
    root_weight = jnp.sqrt(weights)
    return root_weight[..., :, None] * kernel * root_weight[..., None, :]


def draw_left_stats(key, part):
    key = jax.random.fold_in(key, 11)
    return stat_matrix(key, 1.0, 0.9, 64.0)


def draw_right_stats(key, part):
    key = jax.random.fold_in(key, 12)
    return stat_matrix(key, 1.0, 0.9, 64.0)


def draw_refresh(key, part):
    key = jax.random.fold_in(key, 13)
    begin = jax.random.randint(key, (SECTIONS, TENSORS, 1), 0, BLK_T, jnp.int32)
    steps = jnp.arange(NREF, dtype=jnp.int32)
    return ((begin + steps) % BLK_T).astype(jnp.int32)


def raised(values, stream_key, source, target, parts, factor):
    def block_of(dim):
        return (jnp.arange(values.shape[dim]) // (values.shape[dim] // parts)).reshape((-1,) + (1,) * (values.ndim - 1 - dim))

    near = jax.random.permutation(stream_key, parts)[block_of(target)]
    second = (block_of(target) + parts // 2) % parts
    return jnp.where((block_of(source) == near) | (block_of(source) == second), factor * values, values)


def shard_levels(rng, extent, pieces, low, top_value):
    def one(axis_at, shards_of):
        steps = jax.random.uniform(jax.random.fold_in(jax.random.fold_in(rng, 6), axis_at), (shards_of,), jnp.float32, low / len(pieces), top_value / len(pieces))
        return jnp.repeat(jnp.exp(steps), extent[axis_at] // shards_of).reshape((-1,) + (1,) * (len(extent) - axis_at - 1))

    level = one(*pieces[0])
    for cut in pieces[1:]:
        level = level * one(*cut)
    return level


def centred(own_key, dims, scale, bound, pieces=(), kind=jnp.bfloat16):
    values = scale * jax.random.normal(own_key, dims, jnp.float32)
    if pieces:
        values = values * shard_levels(own_key, dims, pieces, -0.22, 0.18)
    return jnp.clip(values, -bound, bound).astype(kind)


def bell_draw_with(stream_key, shape, deviation, limit, cuts, heavy, kind=jnp.bfloat16):
    values = deviation * jax.random.normal(stream_key, shape, jnp.float32)
    if cuts:
        values = values * shard_levels(stream_key, shape, cuts, -0.22, 0.18)
    return jnp.clip(raised(values, jax.random.fold_in(stream_key, 3), *heavy), -limit, limit).astype(kind)


def setup_inputs(seed: int = 0) -> dict:
    key_list = jax.random.split(jax.random.key(seed), 9)
    top_grad = centred(key_list[0], (MICRO, TOKENS, D), 1.0, 6.0, ((1, 32), (2, 4)))
    stash = centred(key_list[1], (SECTIONS, MICRO, TOKENS, D), 1.0, 6.0, ((0, 4), (2, 32), (3, 4)))
    value_grad = bell_draw_with(key_list[2], (SECTIONS, MICRO, TOKENS, KV), 1.0, 6.0, ((0, 4), (2, 32), (3, 4)), (2, 3, 32, 2.75))
    value_weight = centred(key_list[3], (SECTIONS, KV, D), KV ** -0.5, 0.25, ((0, 4), (1, 32), (2, 4)))
    left_stats = draw_left_stats(jax.random.fold_in(key_list[8], 71), 0)
    right_stats = draw_right_stats(jax.random.fold_in(key_list[8], 71), 0)
    refresh = draw_refresh(jax.random.fold_in(key_list[8], 71), 0)
    order = jax.random.permutation(key_list[7], MICRO).astype(jnp.int32)
    return dict(top_grad=top_grad, stash=stash, value_grad=value_grad, value_weight=value_weight, left_stats=left_stats, right_stats=right_stats, refresh=refresh, order=order)


EPS = 1e-06

def inverse_root(statistic):
    order_size = statistic.shape[-1]
    scale = jnp.sqrt(lax.optimization_barrier(jnp.mean(statistic * statistic, axis=(-2, -1), keepdims=True)) + EPS) * order_size
    normed = statistic / scale
    identity = jnp.eye(order_size, dtype=statistic.dtype)
    result = jnp.broadcast_to(identity, statistic.shape)
    for step in range(ITERS):
        factor = (5.0 * identity - normed) * 0.25
        result = jnp.matmul(result, factor, precision=lax.Precision.HIGHEST)
        if step + 1 < ITERS:
            square = jnp.matmul(factor, factor, precision=lax.Precision.HIGHEST)
            fourth = jnp.matmul(square, square, precision=lax.Precision.HIGHEST)
            normed = jnp.matmul(fourth, normed, precision=lax.Precision.HIGHEST)
    return result

def add_group(totals, pair):
    part = lax.dot_general(pair[0], pair[1], (((0,), (0,)), ((), ())), preferred_element_type=jnp.float32)
    rounded = lax.optimization_barrier(part.astype(jnp.bfloat16))
    return (totals + rounded.astype(jnp.float32), None)

def reference(top_grad, stash, value_grad, value_weight, left_stats, right_stats, refresh, order):
    carried = top_grad
    section_grads = [None] * SECTIONS
    for section in reversed(range(SECTIONS)):
        contribution = jnp.dot(value_grad[section].reshape(MICRO * TOKENS, KV), value_weight[section], preferred_element_type=jnp.float32).reshape(MICRO, TOKENS, D)
        carried = (carried.astype(jnp.float32) + contribution).astype(jnp.bfloat16)
        section_grads[section] = carried
    input_grad = jnp.stack(section_grads)
    weight_list, left_list, right_list, root_list = ([], [], [], [])
    for section in range(SECTIONS):
        paired = jnp.take(value_grad[section], order, axis=0)
        grads = paired.reshape(MICRO, GROUPS, TOK_DEV, KV).transpose(1, 0, 2, 3).reshape(GROUPS, MICRO * TOK_DEV, KV)
        inputs = stash[section].reshape(MICRO, GROUPS, TOK_DEV, D).transpose(1, 0, 2, 3).reshape(GROUPS, MICRO * TOK_DEV, D)
        total, _ = lax.scan(add_group, jnp.zeros((KV, D), jnp.float32), (grads, inputs))
        weight_list.append(total)
        rounded = lax.optimization_barrier(total.astype(jnp.bfloat16)).astype(jnp.float32)
        blocks = rounded.reshape(KV, BLOCKS, KV)
        left_gram = jnp.einsum('rbk,sbk->brs', blocks, blocks, precision=lax.Precision.HIGHEST)
        right_gram = jnp.einsum('rbc,rbk->bck', blocks, blocks, precision=lax.Precision.HIGHEST)
        left_now = left_stats[section] + left_gram
        right_now = right_stats[section] + right_gram
        left_list.append(left_now)
        right_list.append(right_now)
        tensor_roots = []
        for tensor_index in range(TENSORS):
            chosen = tensor_index * BLK_T + refresh[section, tensor_index]
            lefts = jnp.take(left_now, chosen, axis=0)
            rights = jnp.take(right_now, chosen, axis=0)
            items = jnp.stack([lefts, rights], axis=1).reshape(2 * NREF, KV, KV)
            tensor_roots.append(inverse_root(items))
        root_list.append(jnp.stack(tensor_roots))
    return (input_grad, jnp.stack(weight_list), jnp.stack(left_list), jnp.stack(right_list), jnp.stack(root_list))
```

```python
import jax
import jax.numpy as jnp
from jax import lax
from jax.sharding import PartitionSpec as P

EPS = 1e-06

NX = 4
NY = 8
X_GROUPS = [[x * NY + y for x in range(NX)] for y in range(NY)]
Y_GROUPS = [[x * NY + y for y in range(NY)] for x in range(NX)]
CHUNKS = 4


def exchange(block, groups):
    return lax.all_to_all(block, "dp", 0, 0, axis_index_groups=groups, tiled=True)


def spread(block, count, groups):
    return exchange(jnp.broadcast_to(block[None], (count, *block.shape)), groups)


def root_rows(stat, row_of):
    size = stat.shape[-1]
    scale = jnp.sqrt(jnp.mean(stat * stat, axis=(-2, -1), keepdims=True) + EPS) * size
    normed = stat / scale
    mine = row_of(normed)
    identity = row_of(jnp.broadcast_to(jnp.eye(size, dtype=jnp.float32), stat.shape))
    matrix = normed.astype(jnp.bfloat16)
    term = mine
    for _ in range(5):
        term = 1.25 * term - 0.25 * jnp.einsum(
            "srk,skc->src",
            term.astype(jnp.bfloat16),
            matrix,
            preferred_element_type=jnp.float32,
        )
    return 0.25 * (6.25 * identity - 1.25 * mine - term)


def per_device(top_grad, stash, value_grad, value_weight, left_stats, right_stats, refresh, order):
    micro, tok_dev, width = top_grad.shape
    rows_own = value_weight.shape[1]
    blocks = left_stats.shape[1]
    kv = left_stats.shape[3]
    tokens = micro * tok_dev
    n_section = lax.axis_size("section")
    section = lax.axis_index("section")
    y_index = lax.axis_index("dp") % NY

    value_full = lax.all_gather(value_grad[0], "tensor", axis=2, tiled=True)

    weight_x = spread(value_weight[0], NX, X_GROUPS)
    weight = lax.all_gather(weight_x, "dp", axis=0, axis_index_groups=Y_GROUPS)
    weight = weight.transpose(1, 0, 2, 3).reshape(kv, width)

    paired = jnp.take(value_full, order, axis=0).reshape(tokens, kv)
    inputs = stash[0].reshape(tokens, width)
    partial = jnp.stack(
        [
            lax.dot_general(
                paired,
                inputs[:, b * kv : (b + 1) * kv],
                (((0,), (0,)), ((), ())),
                preferred_element_type=jnp.float32,
            ).astype(jnp.bfloat16)
            for b in range(blocks)
        ]
    )
    over_x = jnp.sum(exchange(partial, X_GROUPS).astype(jnp.float32), axis=0).astype(jnp.bfloat16)
    by_y = over_x.reshape(NX, NY, rows_own, kv).transpose(1, 0, 2, 3)
    own = jnp.sum(exchange(by_y, Y_GROUPS).astype(jnp.float32), axis=0)
    own_rounded = own.astype(jnp.bfloat16)
    block = spread(own_rounded, NY, Y_GROUPS).transpose(1, 0, 2, 3).reshape(kv, kv)

    stats = jnp.stack([left_stats[0], right_stats[0]], axis=1).astype(jnp.bfloat16)
    stats = exchange(stats, X_GROUPS)
    stats = lax.all_gather(stats, "dp", axis=0, axis_index_groups=Y_GROUPS)
    stats = stats.transpose(2, 1, 0, 3, 4).reshape(2, kv, kv).astype(jnp.float32)

    def row_of(arr):
        view = arr.reshape(2, NX, NY, rows_own, kv)
        picked = lax.dynamic_index_in_dim(view, y_index, 2, keepdims=False)
        return picked.reshape(2, NX * rows_own, kv)

    left_gram = lax.dot_general(
        block, block, (((1,), (1,)), ((), ())), preferred_element_type=jnp.float32
    )
    right_gram = lax.dot_general(
        block, block, (((0,), (0,)), ((), ())), preferred_element_type=jnp.float32
    )
    grams = jnp.stack([left_gram, right_gram])
    roots_mine = root_rows(stats + grams, row_of)
    grams_mine = row_of(grams)
    sent = jnp.concatenate(
        [own_rounded.reshape(1, NX, rows_own, kv)]
        + [a.astype(jnp.bfloat16).reshape(2, NX, rows_own, kv) for a in (grams_mine, roots_mine)],
        axis=0,
    ).transpose(1, 0, 2, 3)
    back = exchange(sent, X_GROUPS).astype(jnp.float32)
    weight_grad = back[:, 0].transpose(1, 0, 2).reshape(rows_own, width)
    new_left = left_stats[0] + back[:, 1]
    new_right = right_stats[0] + back[:, 2]
    roots = jnp.take(back[:, 3:5], refresh[0, 0], axis=0).reshape(-1, rows_own, kv)

    grads_flat = value_full.reshape(tokens, kv)
    top = top_grad.reshape(tokens, width)
    cols = width // CHUNKS
    pieces = []
    for k in range(CHUNKS):
        part = slice(k * cols, (k + 1) * cols)
        contribution = jnp.dot(
            grads_flat, weight[:, part], preferred_element_type=jnp.float32
        )
        held = (top[:, part].astype(jnp.float32) + contribution).astype(jnp.bfloat16)
        for below in range(n_section - 2, -1, -1):
            arrived = lax.ppermute(held, "section", [(below + 1, below)])
            updated = (arrived.astype(jnp.float32) + contribution).astype(jnp.bfloat16)
            held = jnp.where(section == below, updated, held)
        pieces.append(held)
    section_grad = jnp.concatenate(pieces, axis=1).reshape(micro, tok_dev, width)
    return (
        section_grad[None],
        weight_grad[None],
        new_left[None],
        new_right[None],
        roots[None, None],
    )


def solution(mesh):
    return jax.shard_map(
        per_device,
        mesh=mesh,
        in_specs=(
            P(None, "dp", "tensor"),
            P("section", None, "dp", "tensor"),
            P("section", None, "dp", "tensor"),
            P("section", "dp", "tensor"),
            P("section", "tensor", "dp", None),
            P("section", "tensor", "dp", None),
            P("section", "tensor", None),
            P(),
        ),
        out_specs=(
            P("section", None, "dp", "tensor"),
            P("section", "dp", "tensor"),
            P("section", "tensor", "dp", None),
            P("section", "tensor", "dp", None),
            P("section", "tensor", None, "dp", None),
        ),
        check_vma=False,
    )
```

```python
import jax
import jax.numpy as jnp
from jax import lax
from jax.experimental import pallas as pl
from jax.experimental.pallas import tpu as pltpu
from jax.sharding import PartitionSpec as P

EPS = 1e-06

NX = 4
NY = 8
X_GROUPS = [[x * NY + y for x in range(NX)] for y in range(NY)]
Y_GROUPS = [[x * NY + y for y in range(NY)] for x in range(NX)]
CHUNKS = 2
PARAMS = pltpu.CompilerParams(vmem_limit_bytes=40 * 1024 * 1024)


def exchange(block, groups):
    return lax.all_to_all(block, "dp", 0, 0, axis_index_groups=groups, tiled=True)


def spread(block, count, groups):
    return exchange(jnp.broadcast_to(block[None], (count, *block.shape)), groups)


def own_kernel(half, values, near_weight, far_weight, near, far, far_sent):
    rows = values.shape[1]

    def product(weight):
        return jnp.dot(
            values[...],
            weight[...].reshape(rows, weight.shape[-1]),
            preferred_element_type=jnp.float32,
        )

    near[...] = product(near_weight)
    of_far = product(far_weight)
    far[...] = of_far
    far_sent[...] = of_far.astype(jnp.bfloat16)


def own_contribution(half, values, gathered, place, cols):
    tokens, kv = values.shape
    rows_own = kv // (NX * NY)
    result = pl.BlockSpec((tokens, cols), lambda i, h: (0, 0))
    shape = (NY, NX, rows_own, cols)
    return pl.pallas_call(
        own_kernel,
        grid_spec=pltpu.PrefetchScalarGridSpec(
            num_scalar_prefetch=1,
            grid=(1,),
            in_specs=[
                pl.BlockSpec((tokens, kv), lambda i, h: (0, 0)),
                pl.BlockSpec(shape, lambda i, h: (0, 0, h[0], place)),
                pl.BlockSpec(shape, lambda i, h: (0, 0, 1 - h[0], place)),
            ],
            out_specs=[result, result, result],
        ),
        out_shape=[
            jax.ShapeDtypeStruct((tokens, cols), jnp.float32),
            jax.ShapeDtypeStruct((tokens, cols), jnp.float32),
            jax.ShapeDtypeStruct((tokens, cols), jnp.bfloat16),
        ],
        cost_estimate=pl.CostEstimate(
            flops=4 * tokens * kv * cols, bytes_accessed=3 * 1024 * 1024, transcendentals=0
        ),
        compiler_params=PARAMS,
    )(half.reshape(1).astype(jnp.int32), values, gathered, gathered)


def solve_kernel(y_ref, stats, block, sent, rows, left, right, matrix):
    own = stats.shape[2]
    size = block.shape[-1]
    y = y_ref[0]
    for x in range(NX):
        for other in range(NY):
            place = slice((x * NY + other) * own, (x * NY + other + 1) * own)
            rows[place, :] = block[other, x]
            left[place, :] = stats[other, x, :, :size].astype(jnp.float32)
            right[place, :] = stats[other, x, :, size:].astype(jnp.float32)
    whole = rows[...]
    starts = [pl.multiple_of(x * NY * own + y * own, own) for x in range(NX)]

    def mine(ref):
        return jnp.concatenate([ref[pl.ds(start, own), :] for start in starts], axis=0)

    picked = mine(rows)
    for x in range(NX):
        sent[x, 0] = picked[x * own : (x + 1) * own]
    line = lax.broadcasted_iota(jnp.int32, (NX * own, size), 0)
    line = (line // own) * (NY * own) + y * own + line % own
    column = lax.broadcasted_iota(jnp.int32, (NX * own, size), 1)
    identity = jnp.where(line == column, 1.0, 0.0)
    for side, (ref, dims) in enumerate(((left, 1), (right, 0))):
        gram = lax.dot_general(
            whole, whole, (((dims,), (dims,)), ((), ())), preferred_element_type=jnp.float32
        )
        stat = ref[...] + gram
        ref[...] = stat
        now = mine(ref)
        total = jnp.sum(stat * stat, axis=1, keepdims=True)
        total = jnp.sum(total, axis=0, keepdims=True) / (size * size)
        scale = 1.0 / (jnp.sqrt(total + EPS) * size)
        matrix[...] = (stat * scale).astype(jnp.bfloat16)
        first = now * scale
        term = first
        for _ in range(5):
            term = 1.25 * term - 0.25 * jnp.dot(
                term.astype(jnp.bfloat16), matrix[...], preferred_element_type=jnp.float32
            )
        root = 0.25 * (6.25 * identity - 1.25 * first - term)
        root = root.astype(jnp.bfloat16)
        ref[...] = gram
        gram_rows = mine(ref).astype(jnp.bfloat16)
        for x in range(NX):
            part = slice(x * own, (x + 1) * own)
            sent[x, 1 + side] = gram_rows[part]
            sent[x, 3 + side] = root[part]


def solve(y_index, gathered, block):
    own, size = block.shape[2:]
    return pl.pallas_call(
        solve_kernel,
        grid=(1,),
        in_specs=[
            pl.BlockSpec(memory_space=pltpu.SMEM),
            pl.BlockSpec((NY, NX, own, 2 * size), lambda i: (0, 0, 2, 0)),
            pl.BlockSpec(block.shape, lambda i: (0, 0, 0, 0)),
        ],
        out_specs=pl.BlockSpec((NX, 5, own, size), lambda i: (0, 0, 0, 0)),
        out_shape=jax.ShapeDtypeStruct((NX, 5, own, size), jnp.bfloat16),
        scratch_shapes=[
            pltpu.VMEM((size, size), jnp.bfloat16),
            pltpu.VMEM((size, size), jnp.float32),
            pltpu.VMEM((size, size), jnp.float32),
            pltpu.VMEM((size, size), jnp.bfloat16),
        ],
        cost_estimate=pl.CostEstimate(
            flops=3 * 2 * size**3, bytes_accessed=2 * 1024 * 1024, transcendentals=0
        ),
        compiler_params=PARAMS,
    )(y_index.reshape(1).astype(jnp.int32), gathered, block)


def finish_kernel(refresh, back, left_stats, right_stats, weight_grad, new_left, new_right, roots):
    size = back.shape[-1]
    for b in range(NX):
        weight_grad[:, b * size : (b + 1) * size] = back[b, 0].astype(jnp.float32)
        new_left[b] = left_stats[b] + back[b, 1].astype(jnp.float32)
        new_right[b] = right_stats[b] + back[b, 2].astype(jnp.float32)
    for k in range(roots.shape[0] // 2):
        chosen = refresh[k]
        roots[2 * k] = back[chosen, 3].astype(jnp.float32)
        roots[2 * k + 1] = back[chosen, 4].astype(jnp.float32)


def finish(refresh, back, left_stats, right_stats):
    own, size = back.shape[2:]
    picks = 2 * refresh.shape[0]
    shapes = [
        (own, NX * size),
        left_stats.shape,
        right_stats.shape,
        (picks, own, size),
    ]
    vmem = pl.BlockSpec(memory_space=pltpu.VMEM)
    return pl.pallas_call(
        finish_kernel,
        in_specs=[pl.BlockSpec(memory_space=pltpu.SMEM), vmem, vmem, vmem],
        out_specs=[vmem] * 4,
        out_shape=[jax.ShapeDtypeStruct(s, jnp.float32) for s in shapes],
        cost_estimate=pl.CostEstimate(
            flops=1024, bytes_accessed=2 * 1024 * 1024, transcendentals=0
        ),
        compiler_params=PARAMS,
    )(refresh, back, left_stats, right_stats)


def per_device(top_grad, stash, value_grad, value_weight, left_stats, right_stats, refresh, order):
    micro, tok_dev, width = top_grad.shape
    rows_own = value_weight.shape[1]
    blocks = left_stats.shape[1]
    kv = left_stats.shape[3]
    tokens = micro * tok_dev
    section = lax.axis_index("section")
    y_index = lax.axis_index("dp") % NY

    value_full = lax.all_gather(value_grad[0], "tensor", axis=2, tiled=True)

    stats = jnp.concatenate([left_stats[0], right_stats[0]], axis=2).astype(jnp.bfloat16)
    halves = value_weight[0].reshape(rows_own, 2, width // 2).transpose(1, 0, 2)
    halves = jnp.broadcast_to(halves.reshape(1, -1, width // 2), (NX, 2 * rows_own, width // 2))
    first = exchange(jnp.concatenate([halves, stats], axis=1), X_GROUPS)
    gathered = lax.all_gather(first, "dp", axis=0, axis_index_groups=Y_GROUPS)

    paired = jnp.take(value_full, order, axis=0).reshape(tokens, kv)
    inputs = stash[0].reshape(tokens, width)
    partial = jnp.stack(
        [
            lax.dot_general(
                paired,
                inputs[:, b * kv : (b + 1) * kv],
                (((0,), (0,)), ((), ())),
                preferred_element_type=jnp.float32,
            ).astype(jnp.bfloat16)
            for b in range(blocks)
        ]
    )
    over_x = exchange(partial, X_GROUPS)
    over_x = jnp.sum(over_x.astype(jnp.float32), axis=0).astype(jnp.bfloat16)
    by_y = over_x.reshape(NX, NY, rows_own, kv).transpose(1, 0, 2, 3)
    over_y = exchange(by_y, Y_GROUPS)

    value_own = value_full.reshape(tokens, NX, NY, rows_own).transpose(0, 2, 1, 3)
    value_own = value_own.reshape(tokens, kv)
    is_left = (section == 1) | (section == 2)
    cols = width // 2 // CHUNKS
    owns = [
        own_contribution(jnp.where(is_left, 0, 1), value_own, gathered, k, cols)
        for k in range(CHUNKS)
    ]
    over_y, _ = lax.optimization_barrier((over_y, owns))
    own = jnp.sum(over_y.astype(jnp.float32), axis=0)
    block = spread(own.astype(jnp.bfloat16), NY, Y_GROUPS)

    top = top_grad.reshape(tokens, 2, width // 2)
    top_near = jnp.where(is_left, top[:, 0], top[:, 1])
    top_far = jnp.where(is_left, top[:, 1], top[:, 0])
    f32, bf16 = jnp.float32, jnp.bfloat16
    mates = [lax.ppermute(sent, "section", [(3, 2), (2, 3), (1, 0)]) for _, _, sent in owns]
    helds, bases, seconds = [], [], []
    for k, (near, _, _) in enumerate(owns):
        mate = mates[k]
        if k:
            mate, _ = lax.optimization_barrier((mate, helds[-1]))
        base = near + mate.astype(f32)
        bases.append(base)
        helds.append((top_near[:, k * cols : (k + 1) * cols].astype(f32) + base).astype(bf16))
        seconds.append(lax.ppermute(helds[-1], "section", [(2, 1), (3, 0)]))
    nears, fars = [], []
    last = helds[-1]
    for k, (near, far, _) in enumerate(owns):
        part = slice(k * cols, (k + 1) * cols)
        second, _ = lax.optimization_barrier((seconds[k], last))
        updated = (second.astype(f32) + bases[k]).astype(bf16)
        alone = (top_near[:, part].astype(f32) + near).astype(bf16)
        passed = jnp.where(section == 0, second, jnp.where(section == 1, updated, helds[k]))
        last = passed
        nears.append(
            jnp.where(section == 3, alone, jnp.where(section == 2, helds[k], updated))
        )
        third = lax.ppermute(passed, "section", [(1, 0), (0, 1), (3, 2)])
        fars.append((third, far, top_far[:, part]))

    block, _ = lax.optimization_barrier((block, helds))
    sent = solve(y_index, gathered, block)
    fars, _ = lax.optimization_barrier((fars, sent))
    back = exchange(sent, X_GROUPS)
    weight_grad, new_left, new_right, roots = finish(
        refresh[0, 0], back, left_stats[0], right_stats[0]
    )
    fars = [
        jnp.where(
            section == 2,
            third,
            (jnp.where(section == 3, above, third).astype(f32) + far).astype(bf16),
        )
        for third, far, above in fars
    ]
    near, far = jnp.concatenate(nears, axis=1), jnp.concatenate(fars, axis=1)
    section_grad = jnp.concatenate(
        [jnp.where(is_left, near, far), jnp.where(is_left, far, near)], axis=1
    ).reshape(micro, tok_dev, width)
    return (
        section_grad[None],
        weight_grad[None],
        new_left[None],
        new_right[None],
        roots[None, None],
    )


def solution(mesh):
    return jax.shard_map(
        per_device,
        mesh=mesh,
        in_specs=(
            P(None, "dp", "tensor"),
            P("section", None, "dp", "tensor"),
            P("section", None, "dp", "tensor"),
            P("section", "dp", "tensor"),
            P("section", "tensor", "dp", None),
            P("section", "tensor", "dp", None),
            P("section", "tensor", None),
            P(),
        ),
        out_specs=(
            P("section", None, "dp", "tensor"),
            P("section", "dp", "tensor"),
            P("section", "tensor", "dp", None),
            P("section", "tensor", "dp", None),
            P("section", "tensor", None, "dp", None),
        ),
        check_vma=False,
    )
```

```python
import jax
import jax.numpy as jnp
from jax import lax
from jax.experimental import pallas as pl
from jax.experimental.pallas import tpu as pltpu
from jax.sharding import PartitionSpec as P

EPS = 1e-06

NX = 4
NY = 8
X_GROUPS = [[x * NY + y for x in range(NX)] for y in range(NY)]
Y_GROUPS = [[x * NY + y for y in range(NY)] for x in range(NX)]
PIECE = 256
SPLIT = 3
PARAMS = pltpu.CompilerParams(vmem_limit_bytes=40 * 1024 * 1024)


def exchange(block, groups):
    return lax.all_to_all(block, "dp", 0, 0, axis_index_groups=groups, tiled=True)


def pack_kernel(weight, left, right, packed):
    own = weight.shape[0]
    per_half = weight.shape[1] // (2 * PIECE)
    rest = per_half - SPLIT

    def put(x, group, piece):
        packed[x, group * own : (group + 1) * own, :] = piece

    for h in range(2):
        for p in range(per_half):
            group = h * SPLIT + p if p < SPLIT else 2 * SPLIT + h * rest + p - SPLIT
            column = (h * per_half + p) * PIECE
            for x in range(NX):
                put(x, group, weight[:, column : column + PIECE])
    group = 2 * per_half
    for ref in (left, right):
        for p in range(ref.shape[2] // PIECE):
            for x in range(NX):
                put(x, group, ref[x, :, p * PIECE : (p + 1) * PIECE].astype(jnp.bfloat16))
            group += 1


def pack(weight, left, right):
    own, width = weight.shape
    rows = own * (width + 2 * left.shape[2]) // PIECE
    return whole_call(
        pack_kernel, jax.ShapeDtypeStruct((NX, rows, PIECE), jnp.bfloat16), weight, left, right
    )


def over_x_kernel(parts, result):
    own = result.shape[2]
    for x in range(NX):
        for y in range(NY):
            place = slice((x * NY + y) * own, (x * NY + y + 1) * own)
            total = parts[0, place, :].astype(jnp.float32)
            for k in range(1, NX):
                total += parts[k, place, :].astype(jnp.float32)
            result[y, x] = total.astype(jnp.bfloat16)


def over_y_kernel(parts, result):
    total = parts[0].astype(jnp.float32)
    for k in range(1, NY):
        total += parts[k].astype(jnp.float32)
    total = total.astype(jnp.bfloat16)
    for k in range(NY):
        result[k] = total


def whole_call(kernel, out_shape, *operands):
    vmem = pl.BlockSpec(memory_space=pltpu.VMEM)
    return pl.pallas_call(
        kernel,
        in_specs=[vmem] * len(operands),
        out_specs=vmem,
        out_shape=out_shape,
        cost_estimate=pl.CostEstimate(
            flops=1024, bytes_accessed=2 * 1024 * 1024, transcendentals=0
        ),
        compiler_params=PARAMS,
    )(*operands)


def own_kernel(half, values, *refs):
    rows = values.shape[1]
    count = (len(refs) - 3) // 2
    near, far, far_sent = refs[2 * count :]
    for p in range(count):
        place = slice(p * PIECE, (p + 1) * PIECE)
        of_near, of_far = [
            jnp.dot(values[...], weight[...].reshape(rows, PIECE), preferred_element_type=jnp.float32)
            for weight in (refs[p], refs[count + p])
        ]
        near[:, place] = of_near
        far[:, place] = of_far
        far_sent[:, place] = of_far.astype(jnp.bfloat16)


def own_contribution(half, values, pieces):
    tokens, kv = values.shape
    shape = (NY, NX, kv // (NX * NY), PIECE)
    width = len(pieces) * PIECE
    result = pl.BlockSpec((tokens, width), lambda i, h: (0, 0))

    def near(first, stride):
        return pl.BlockSpec(shape, lambda i, h: (0, 0, first + h[0] * stride, 0))

    def far(first, stride):
        return pl.BlockSpec(shape, lambda i, h: (0, 0, first + (1 - h[0]) * stride, 0))

    arrays = [array for array, _, _ in pieces]
    return pl.pallas_call(
        own_kernel,
        grid_spec=pltpu.PrefetchScalarGridSpec(
            num_scalar_prefetch=1,
            grid=(1,),
            in_specs=[pl.BlockSpec((tokens, kv), lambda i, h: (0, 0))]
            + [near(first, stride) for _, first, stride in pieces]
            + [far(first, stride) for _, first, stride in pieces],
            out_specs=[result, result, result],
        ),
        out_shape=[
            jax.ShapeDtypeStruct((tokens, width), jnp.float32),
            jax.ShapeDtypeStruct((tokens, width), jnp.float32),
            jax.ShapeDtypeStruct((tokens, width), jnp.bfloat16),
        ],
        cost_estimate=pl.CostEstimate(
            flops=4 * tokens * kv * width,
            bytes_accessed=len(pieces) * 1536 * 1024,
            transcendentals=0,
        ),
        compiler_params=PARAMS,
    )(half.reshape(1).astype(jnp.int32), values, *arrays, *arrays)


def solve_kernel(y_ref, stats, block, sent, rows, left, right, matrix):
    own, size = block.shape[2:]
    y = y_ref[0]
    for x in range(NX):
        for other in range(NY):
            place = slice((x * NY + other) * own, (x * NY + other + 1) * own)
            rows[place, :] = block[other, x]
            for side, ref in enumerate((left, right)):
                for piece in range(size // PIECE):
                    group = side * (size // PIECE) + piece
                    ref[place, piece * PIECE : (piece + 1) * PIECE] = stats[
                        other, x, group * own : (group + 1) * own, :
                    ].astype(jnp.float32)
    whole = rows[...]
    starts = [pl.multiple_of(x * NY * own + y * own, own) for x in range(NX)]

    def mine(ref):
        return jnp.concatenate([ref[pl.ds(start, own), :] for start in starts], axis=0)

    picked = mine(rows)
    for x in range(NX):
        sent[x, 0] = picked[x * own : (x + 1) * own]
    line = lax.broadcasted_iota(jnp.int32, (NX * own, size), 0)
    line = (line // own) * (NY * own) + y * own + line % own
    column = lax.broadcasted_iota(jnp.int32, (NX * own, size), 1)
    identity = jnp.where(line == column, 1.0, 0.0)
    for side, (ref, dims) in enumerate(((left, 1), (right, 0))):
        gram = lax.dot_general(
            whole, whole, (((dims,), (dims,)), ((), ())), preferred_element_type=jnp.float32
        )
        stat = ref[...] + gram
        ref[...] = stat
        now = mine(ref)
        total = jnp.sum(stat * stat, axis=1, keepdims=True)
        total = jnp.sum(total, axis=0, keepdims=True) / (size * size)
        scale = 1.0 / (jnp.sqrt(total + EPS) * size)
        matrix[...] = (stat * scale).astype(jnp.bfloat16)
        first = now * scale
        term = first
        for _ in range(5):
            term = 1.25 * term - 0.25 * jnp.dot(
                term.astype(jnp.bfloat16), matrix[...], preferred_element_type=jnp.float32
            )
        root = 0.25 * (6.25 * identity - 1.25 * first - term)
        root = root.astype(jnp.bfloat16)
        ref[...] = gram
        gram_rows = mine(ref).astype(jnp.bfloat16)
        for x in range(NX):
            part = slice(x * own, (x + 1) * own)
            sent[x, 1 + side] = gram_rows[part]
            sent[x, 3 + side] = root[part]


def solve(y_index, gathered, block):
    own, size = block.shape[2:]
    return pl.pallas_call(
        solve_kernel,
        grid=(1,),
        in_specs=[
            pl.BlockSpec(memory_space=pltpu.SMEM),
            pl.BlockSpec((NY, NX, 2 * own * size // PIECE, PIECE), lambda i: (0, 0, 0, 0)),
            pl.BlockSpec(block.shape, lambda i: (0, 0, 0, 0)),
        ],
        out_specs=pl.BlockSpec((NX, 5, own, size), lambda i: (0, 0, 0, 0)),
        out_shape=jax.ShapeDtypeStruct((NX, 5, own, size), jnp.bfloat16),
        scratch_shapes=[
            pltpu.VMEM((size, size), jnp.bfloat16),
            pltpu.VMEM((size, size), jnp.float32),
            pltpu.VMEM((size, size), jnp.float32),
            pltpu.VMEM((size, size), jnp.bfloat16),
        ],
        cost_estimate=pl.CostEstimate(
            flops=3 * 2 * size**3, bytes_accessed=2 * 1024 * 1024, transcendentals=0
        ),
        compiler_params=PARAMS,
    )(y_index.reshape(1).astype(jnp.int32), gathered, block)


def finish_kernel(refresh, back, left_stats, right_stats, weight_grad, new_left, new_right, roots):
    size = back.shape[-1]
    for b in range(NX):
        weight_grad[:, b * size : (b + 1) * size] = back[b, 0].astype(jnp.float32)
        new_left[b] = left_stats[b] + back[b, 1].astype(jnp.float32)
        new_right[b] = right_stats[b] + back[b, 2].astype(jnp.float32)
    for k in range(roots.shape[0] // 2):
        chosen = refresh[k]
        roots[2 * k] = back[chosen, 3].astype(jnp.float32)
        roots[2 * k + 1] = back[chosen, 4].astype(jnp.float32)


def finish(refresh, back, left_stats, right_stats):
    own, size = back.shape[2:]
    picks = 2 * refresh.shape[0]
    shapes = [
        (own, NX * size),
        left_stats.shape,
        right_stats.shape,
        (picks, own, size),
    ]
    vmem = pl.BlockSpec(memory_space=pltpu.VMEM)
    return pl.pallas_call(
        finish_kernel,
        in_specs=[pl.BlockSpec(memory_space=pltpu.SMEM), vmem, vmem, vmem],
        out_specs=[vmem] * 4,
        out_shape=[jax.ShapeDtypeStruct(s, jnp.float32) for s in shapes],
        cost_estimate=pl.CostEstimate(
            flops=1024, bytes_accessed=2 * 1024 * 1024, transcendentals=0
        ),
        compiler_params=PARAMS,
    )(refresh, back, left_stats, right_stats)


def per_device(top_grad, stash, value_grad, value_weight, left_stats, right_stats, refresh, order):
    micro, tok_dev, width = top_grad.shape
    rows_own = value_weight.shape[1]
    blocks = left_stats.shape[1]
    kv = left_stats.shape[3]
    tokens = micro * tok_dev
    section = lax.axis_index("section")
    y_index = lax.axis_index("dp") % NY

    value_full = lax.all_gather(value_grad[0], "tensor", axis=2, tiled=True)

    per_half = width // (2 * PIECE)
    early, late = 2 * SPLIT * rows_own, 2 * per_half * rows_own
    first = exchange(pack(value_weight[0], left_stats[0], right_stats[0]), X_GROUPS)
    first, value_full = lax.optimization_barrier((first, value_full))
    gathered = lax.all_gather(first[:, :early], "dp", axis=0, axis_index_groups=Y_GROUPS)

    paired = jnp.take(value_full, order, axis=0).reshape(tokens, kv)
    inputs = stash[0].reshape(tokens, width)
    partial = jnp.stack(
        [
            lax.dot_general(
                paired,
                inputs[:, b * kv : (b + 1) * kv],
                (((0,), (0,)), ((), ())),
                preferred_element_type=jnp.float32,
            ).astype(jnp.bfloat16)
            for b in range(blocks)
        ]
    )
    over_x = exchange(partial, X_GROUPS)
    last, _ = lax.optimization_barrier((first[:, early:late], partial))
    last = lax.all_gather(last, "dp", axis=0, axis_index_groups=Y_GROUPS)

    value_own = value_full.reshape(tokens, NX, NY, rows_own).transpose(0, 2, 1, 3)
    value_own = value_own.reshape(tokens, kv)
    is_left = (section == 1) | (section == 2)
    half = jnp.where(is_left, 0, 1)
    pieces = [(gathered, p, SPLIT) for p in range(SPLIT)] + [(last, 0, 1)]
    owns = [own_contribution(half, value_own, part) for part in (pieces[:2], pieces[2:])]
    to_mate = [(3, 2), (2, 3), (1, 0)]
    mates = [lax.ppermute(owns[0][2], "section", to_mate)]

    stats, _ = lax.optimization_barrier((first[:, late:], gathered))
    stats = lax.all_gather(stats, "dp", axis=0, axis_index_groups=Y_GROUPS)
    top = top_grad.reshape(tokens, 2, width // 2)
    top_near = jnp.where(is_left, top[:, 0], top[:, 1])
    top_far = jnp.where(is_left, top[:, 1], top[:, 0])
    over_x, _ = lax.optimization_barrier((over_x, (last, top_near, top_far, value_own)))
    split_shape = jax.ShapeDtypeStruct((NY, NX, rows_own, kv), jnp.bfloat16)
    by_y = whole_call(over_x_kernel, split_shape, over_x)
    over_y = exchange(by_y, Y_GROUPS)

    f32, bf16 = jnp.float32, jnp.bfloat16
    parts = [slice(0, 2 * PIECE), slice(2 * PIECE, 4 * PIECE)]

    def hold(k, mate):
        base = owns[k][0] + mate.astype(f32)
        return base, (top_near[:, parts[k]].astype(f32) + base).astype(bf16)

    def forward(k, second, base, held):
        updated = (second.astype(f32) + base).astype(bf16)
        alone = (top_near[:, parts[k]].astype(f32) + owns[k][0]).astype(bf16)
        passed = jnp.where(section == 0, second, jnp.where(section == 1, updated, held))
        near = jnp.where(section == 3, alone, jnp.where(section == 2, held, updated))
        return passed, near

    to_lower = [(2, 1), (3, 0)]
    to_other = [(1, 0), (0, 1), (3, 2)]
    over_y, _ = lax.optimization_barrier((over_y, owns))
    own = whole_call(over_y_kernel, split_shape, over_y)
    block = exchange(own, Y_GROUPS)

    mate, _ = lax.optimization_barrier((mates[0], own))
    base_0, held_0 = hold(0, mate)
    second_0 = lax.ppermute(held_0, "section", to_lower)

    far_1, _ = lax.optimization_barrier((owns[1][2], held_0))
    mates.append(lax.ppermute(far_1, "section", to_mate))

    second_0, _ = lax.optimization_barrier((second_0, own))
    passed_0, near_0 = forward(0, second_0, base_0, held_0)
    third_0 = lax.ppermute(passed_0, "section", to_other)

    mate, _ = lax.optimization_barrier((mates[1], passed_0))
    base_1, held_1 = hold(1, mate)
    second_1 = lax.ppermute(held_1, "section", to_lower)

    block, _ = lax.optimization_barrier((block, held_1))
    sent = solve(y_index, stats, block)

    second_1, _ = lax.optimization_barrier((second_1, sent))
    passed_1, near_1 = forward(1, second_1, base_1, held_1)
    third_1 = lax.ppermute(passed_1, "section", to_other)
    nears = [near_0, near_1]
    thirds, _ = lax.optimization_barrier(([third_0, third_1], passed_1))
    fars = [
        (third, owns[k][1], top_far[:, parts[k]]) for k, third in enumerate(thirds)
    ]
    back = exchange(sent, X_GROUPS)
    weight_grad, new_left, new_right, roots = finish(
        refresh[0, 0], back, left_stats[0], right_stats[0]
    )
    fars = [
        jnp.where(
            section == 2,
            third,
            (jnp.where(section == 3, above, third).astype(f32) + far).astype(bf16),
        )
        for third, far, above in fars
    ]
    near, far = jnp.concatenate(nears, axis=1), jnp.concatenate(fars, axis=1)
    section_grad = jnp.concatenate(
        [jnp.where(is_left, near, far), jnp.where(is_left, far, near)], axis=1
    ).reshape(micro, tok_dev, width)
    return (
        section_grad[None],
        weight_grad[None],
        new_left[None],
        new_right[None],
        roots[None, None],
    )


def solution(mesh):
    return jax.shard_map(
        per_device,
        mesh=mesh,
        in_specs=(
            P(None, "dp", "tensor"),
            P("section", None, "dp", "tensor"),
            P("section", None, "dp", "tensor"),
            P("section", "dp", "tensor"),
            P("section", "tensor", "dp", None),
            P("section", "tensor", "dp", None),
            P("section", "tensor", None),
            P(),
        ),
        out_specs=(
            P("section", None, "dp", "tensor"),
            P("section", "dp", "tensor"),
            P("section", "tensor", "dp", None),
            P("section", "tensor", "dp", None),
            P("section", "tensor", None, "dp", None),
        ),
        check_vma=False,
    )
```

```python
import functools

import jax
import jax.numpy as jnp
from jax import lax
from jax.experimental import pallas as pl
from jax.experimental.pallas import tpu as pltpu
from jax.sharding import PartitionSpec as P

EPS = 1e-06

NX = 4
NY = 8
X_GROUPS = [[x * NY + y for x in range(NX)] for y in range(NY)]
Y_GROUPS = [[x * NY + y for y in range(NY)] for x in range(NX)]
PIECE = 256
SPLIT = 3
PARAMS = pltpu.CompilerParams(vmem_limit_bytes=40 * 1024 * 1024)
WIDE = pltpu.CompilerParams(vmem_limit_bytes=56 * 1024 * 1024)


def exchange(block, groups):
    return lax.all_to_all(block, "dp", 0, 0, axis_index_groups=groups, tiled=True)


def pack_kernel(weight, left, right, packed):
    own = weight.shape[0]
    per_half = weight.shape[1] // (2 * PIECE)
    rest = per_half - SPLIT

    def put(x, group, piece):
        packed[x, group * own : (group + 1) * own, :] = piece

    group = 0
    for ref in (left, right):
        for p in range(ref.shape[2] // PIECE):
            for x in range(NX):
                put(x, group, ref[x, :, p * PIECE : (p + 1) * PIECE].astype(jnp.bfloat16))
            group += 1
    for h in range(2):
        for p in range(per_half):
            place = h * SPLIT + p if p < SPLIT else 2 * SPLIT + h * rest + p - SPLIT
            column = (h * per_half + p) * PIECE
            for x in range(NX):
                put(x, group + place, weight[:, column : column + PIECE])


def pack(weight, left, right):
    own, width = weight.shape
    rows = own * (width + 2 * left.shape[2]) // PIECE
    return pl.pallas_call(
        pack_kernel,
        grid=(1,),
        in_specs=[
            pl.BlockSpec(weight.shape, lambda i: (0, 0)),
            pl.BlockSpec(left.shape, lambda i: (0, 0, 0)),
            pl.BlockSpec(right.shape, lambda i: (0, 0, 0)),
        ],
        out_specs=pl.BlockSpec((NX, rows, PIECE), lambda i: (0, 0, 0)),
        out_shape=jax.ShapeDtypeStruct((NX, rows, PIECE), jnp.bfloat16),
        cost_estimate=pl.CostEstimate(
            flops=1024, bytes_accessed=1024 * 1024, transcendentals=0
        ),
        compiler_params=WIDE,
    )(weight, left, right)


def partial_kernel(order, values, inputs, result):
    total = 0.0
    for k in range(inputs.shape[0]):
        total += lax.dot_general(
            values[order[k]],
            inputs[k],
            (((0,), (0,)), ((), ())),
            preferred_element_type=jnp.float32,
        )
    result[0] = total.astype(jnp.bfloat16)


def partial_gradient(order, values, inputs):
    micro, tokens, kv = values.shape
    blocks = inputs.shape[2] // kv
    return pl.pallas_call(
        partial_kernel,
        grid_spec=pltpu.PrefetchScalarGridSpec(
            num_scalar_prefetch=1,
            grid=(blocks,),
            in_specs=[
                pl.BlockSpec((micro, tokens, kv), lambda b, o: (0, 0, 0)),
                pl.BlockSpec((micro, tokens, kv), lambda b, o: (0, 0, b)),
            ],
            out_specs=pl.BlockSpec((1, kv, kv), lambda b, o: (b, 0, 0)),
        ),
        out_shape=jax.ShapeDtypeStruct((blocks, kv, kv), jnp.bfloat16),
        cost_estimate=pl.CostEstimate(
            flops=2 * micro * tokens * kv * kv * blocks,
            bytes_accessed=3 * 1024 * 1024,
            transcendentals=0,
        ),
        compiler_params=PARAMS,
    )(order, values, inputs)


def over_x_kernel(parts, result):
    own = result.shape[2]
    for x in range(NX):
        for y in range(NY):
            place = slice((x * NY + y) * own, (x * NY + y + 1) * own)
            total = parts[0, place, :].astype(jnp.float32)
            for k in range(1, NX):
                total += parts[k, place, :].astype(jnp.float32)
            result[y, x] = total.astype(jnp.bfloat16)


def over_y_kernel(parts, result):
    total = parts[0].astype(jnp.float32)
    for k in range(1, NY):
        total += parts[k].astype(jnp.float32)
    total = total.astype(jnp.bfloat16)
    for k in range(NY):
        result[k] = total


def whole_call(kernel, out_shape, *operands):
    vmem = pl.BlockSpec(memory_space=pltpu.VMEM)
    return pl.pallas_call(
        kernel,
        in_specs=[vmem] * len(operands),
        out_specs=vmem,
        out_shape=out_shape,
        cost_estimate=pl.CostEstimate(
            flops=1024, bytes_accessed=2 * 1024 * 1024, transcendentals=0
        ),
        compiler_params=PARAMS,
    )(*operands)


def own_kernel(half, values, *refs):
    rows = values.shape[1]
    count = (len(refs) - 3) // 2
    near, far, far_sent = refs[2 * count :]
    for p in range(count):
        place = slice(p * PIECE, (p + 1) * PIECE)
        of_near, of_far = [
            jnp.dot(values[...], weight[...].reshape(rows, PIECE), preferred_element_type=jnp.float32)
            for weight in (refs[p], refs[count + p])
        ]
        near[:, place] = of_near
        far[:, place] = of_far
        far_sent[:, place] = of_far.astype(jnp.bfloat16)


def own_contribution(half, values, pieces):
    tokens, kv = values.shape
    shape = (NY, NX, kv // (NX * NY), PIECE)
    width = len(pieces) * PIECE
    result = pl.BlockSpec((tokens, width), lambda i, h: (0, 0))

    def near(first, stride):
        return pl.BlockSpec(shape, lambda i, h: (0, 0, first + h[0] * stride, 0))

    def far(first, stride):
        return pl.BlockSpec(shape, lambda i, h: (0, 0, first + (1 - h[0]) * stride, 0))

    arrays = [array for array, _, _ in pieces]
    return pl.pallas_call(
        own_kernel,
        grid_spec=pltpu.PrefetchScalarGridSpec(
            num_scalar_prefetch=1,
            grid=(1,),
            in_specs=[pl.BlockSpec((tokens, kv), lambda i, h: (0, 0))]
            + [near(first, stride) for _, first, stride in pieces]
            + [far(first, stride) for _, first, stride in pieces],
            out_specs=[result, result, result],
        ),
        out_shape=[
            jax.ShapeDtypeStruct((tokens, width), jnp.float32),
            jax.ShapeDtypeStruct((tokens, width), jnp.float32),
            jax.ShapeDtypeStruct((tokens, width), jnp.bfloat16),
        ],
        cost_estimate=pl.CostEstimate(
            flops=4 * tokens * kv * width,
            bytes_accessed=len(pieces) * 1536 * 1024,
            transcendentals=0,
        ),
        compiler_params=PARAMS,
    )(half.reshape(1).astype(jnp.int32), values, *arrays, *arrays)


def solve_kernel(y_ref, left_0, left_1, right_0, right_1, block, sent, rows, left, right, matrix):
    own, size = block.shape[2:]
    y = y_ref[0]
    for x in range(NX):
        for other in range(NY):
            place = slice((x * NY + other) * own, (x * NY + other + 1) * own)
            rows[place, :] = block[other, x]
            for ref, pieces in ((left, (left_0, left_1)), (right, (right_0, right_1))):
                for p, piece in enumerate(pieces):
                    ref[place, p * PIECE : (p + 1) * PIECE] = piece[other, x].astype(jnp.float32)
    whole = rows[...]
    starts = [pl.multiple_of(x * NY * own + y * own, own) for x in range(NX)]

    def mine(ref):
        return jnp.concatenate([ref[pl.ds(start, own), :] for start in starts], axis=0)

    picked = mine(rows)
    for x in range(NX):
        sent[x, 0] = picked[x * own : (x + 1) * own]
    line = lax.broadcasted_iota(jnp.int32, (NX * own, size), 0)
    line = (line // own) * (NY * own) + y * own + line % own
    column = lax.broadcasted_iota(jnp.int32, (NX * own, size), 1)
    identity = jnp.where(line == column, 1.0, 0.0)
    for side, (ref, dims) in enumerate(((left, 1), (right, 0))):
        gram = lax.dot_general(
            whole, whole, (((dims,), (dims,)), ((), ())), preferred_element_type=jnp.float32
        )
        stat = ref[...] + gram
        ref[...] = stat
        now = mine(ref)
        total = jnp.sum(stat * stat, axis=1, keepdims=True)
        total = jnp.sum(total, axis=0, keepdims=True) / (size * size)
        scale = 1.0 / (jnp.sqrt(total + EPS) * size)
        matrix[...] = (stat * scale).astype(jnp.bfloat16)
        first = now * scale
        term = first
        for _ in range(5):
            term = 1.25 * term - 0.25 * jnp.dot(
                term.astype(jnp.bfloat16), matrix[...], preferred_element_type=jnp.float32
            )
        root = 0.25 * (6.25 * identity - 1.25 * first - term)
        root = root.astype(jnp.bfloat16)
        ref[...] = gram
        gram_rows = mine(ref).astype(jnp.bfloat16)
        for x in range(NX):
            part = slice(x * own, (x + 1) * own)
            sent[x, 1 + side] = gram_rows[part]
            sent[x, 3 + side] = root[part]


def group_place(group, i):
    return 0, 0, group, 0


def solve(y_index, gathered, block):
    own, size = block.shape[2:]
    return pl.pallas_call(
        solve_kernel,
        grid=(1,),
        in_specs=[
            pl.BlockSpec(memory_space=pltpu.SMEM),
            *[
                pl.BlockSpec((NY, NX, own, PIECE), functools.partial(group_place, g))
                for g in range(4)
            ],
            pl.BlockSpec(block.shape, lambda i: (0, 0, 0, 0)),
        ],
        out_specs=pl.BlockSpec((NX, 5, own, size), lambda i: (0, 0, 0, 0)),
        out_shape=jax.ShapeDtypeStruct((NX, 5, own, size), jnp.bfloat16),
        scratch_shapes=[
            pltpu.VMEM((size, size), jnp.bfloat16),
            pltpu.VMEM((size, size), jnp.float32),
            pltpu.VMEM((size, size), jnp.float32),
            pltpu.VMEM((size, size), jnp.bfloat16),
        ],
        cost_estimate=pl.CostEstimate(
            flops=3 * 2 * size**3, bytes_accessed=2 * 1024 * 1024, transcendentals=0
        ),
        compiler_params=PARAMS,
    )(y_index.reshape(1).astype(jnp.int32), *[gathered] * 4, block)


def finish_kernel(refresh, back, left_stats, right_stats, weight_grad, new_left, new_right, roots):
    size = back.shape[-1]
    for b in range(NX):
        weight_grad[:, b * size : (b + 1) * size] = back[b, 0].astype(jnp.float32)
        new_left[b] = left_stats[b] + back[b, 1].astype(jnp.float32)
        new_right[b] = right_stats[b] + back[b, 2].astype(jnp.float32)
    for k in range(roots.shape[0] // 2):
        chosen = refresh[k]
        roots[2 * k] = back[chosen, 3].astype(jnp.float32)
        roots[2 * k + 1] = back[chosen, 4].astype(jnp.float32)


def finish(refresh, back, left_stats, right_stats):
    own, size = back.shape[2:]
    picks = 2 * refresh.shape[0]
    shapes = [
        (own, NX * size),
        left_stats.shape,
        right_stats.shape,
        (picks, own, size),
    ]
    vmem = pl.BlockSpec(memory_space=pltpu.VMEM)
    return pl.pallas_call(
        finish_kernel,
        in_specs=[pl.BlockSpec(memory_space=pltpu.SMEM), vmem, vmem, vmem],
        out_specs=[vmem] * 4,
        out_shape=[jax.ShapeDtypeStruct(s, jnp.float32) for s in shapes],
        cost_estimate=pl.CostEstimate(
            flops=1024, bytes_accessed=2 * 1024 * 1024, transcendentals=0
        ),
        compiler_params=PARAMS,
    )(refresh, back, left_stats, right_stats)


def per_device(top_grad, stash, value_grad, value_weight, left_stats, right_stats, refresh, order):
    micro, tok_dev, width = top_grad.shape
    rows_own = value_weight.shape[1]
    kv = left_stats.shape[3]
    tokens = micro * tok_dev
    section = lax.axis_index("section")
    y_index = lax.axis_index("dp") % NY

    value_full = lax.all_gather(value_grad[0], "tensor", axis=2, tiled=True)

    per_half = width // (2 * PIECE)
    groups = 2 * kv // PIECE
    early = (groups + 2 * SPLIT) * rows_own
    first = exchange(pack(value_weight[0], left_stats[0], right_stats[0]), X_GROUPS)
    first, value_full = lax.optimization_barrier((first, value_full))
    late = groups * rows_own
    gathered = lax.all_gather(first[:, late:early], "dp", axis=0, axis_index_groups=Y_GROUPS)
    stats, _ = lax.optimization_barrier((first[:, :late], gathered))
    stats = lax.all_gather(stats, "dp", axis=0, axis_index_groups=Y_GROUPS)

    partial = partial_gradient(order, value_full, stash[0])
    over_x = exchange(partial, X_GROUPS)
    last, _ = lax.optimization_barrier((first[:, early:], partial))
    last = lax.all_gather(last, "dp", axis=0, axis_index_groups=Y_GROUPS)

    value_own = value_full.reshape(tokens, NX, NY, rows_own).transpose(0, 2, 1, 3)
    value_own = value_own.reshape(tokens, kv)
    is_left = (section == 1) | (section == 2)
    half = jnp.where(is_left, 0, 1)
    pieces = [(gathered, p, SPLIT) for p in range(SPLIT)] + [(last, 0, 1)]
    owns = [own_contribution(half, value_own, part) for part in (pieces[:2], pieces[2:])]
    to_mate = [(3, 2), (2, 3), (1, 0)]
    mates = [lax.ppermute(owns[0][2], "section", to_mate)]

    top = top_grad.reshape(tokens, width)
    cols = 2 * PIECE
    left_top, right_top = [
        [top[:, start + k * cols : start + (k + 1) * cols] for k in range(2)]
        for start in (0, width // 2)
    ]
    top_near = [jnp.where(is_left, a, b) for a, b in zip(left_top, right_top)]
    top_far = [jnp.where(is_left, b, a) for a, b in zip(left_top, right_top)]
    over_x, _ = lax.optimization_barrier((over_x, (last, top_near, top_far, value_own)))
    split_shape = jax.ShapeDtypeStruct((NY, NX, rows_own, kv), jnp.bfloat16)
    by_y = whole_call(over_x_kernel, split_shape, over_x)
    over_y = exchange(by_y, Y_GROUPS)

    f32, bf16 = jnp.float32, jnp.bfloat16

    def hold(k, mate):
        return (top_near[k].astype(f32) + (owns[k][0] + mate.astype(f32))).astype(bf16)

    def update(second, near, mate):
        return (second.astype(f32) + (near + mate.astype(f32))).astype(bf16)

    def forward(k, second, mate, held):
        updated = update(second, owns[k][0], mate)
        return jnp.where(section == 0, second, jnp.where(section == 1, updated, held))

    def finished(k, second, mate, held, after):
        second, mate, near, _ = lax.optimization_barrier((second, mate, owns[k][0], after))
        alone = (top_near[k].astype(f32) + near).astype(bf16)
        updated = update(second, near, mate)
        return jnp.where(section == 3, alone, jnp.where(section == 2, held, updated))

    to_lower = [(2, 1), (3, 0)]
    to_other = [(1, 0), (0, 1), (3, 2)]
    over_y, _ = lax.optimization_barrier((over_y, owns))
    own = whole_call(over_y_kernel, split_shape, over_y)
    block = exchange(own, Y_GROUPS)

    mate_0, _ = lax.optimization_barrier((mates[0], own))
    held_0 = hold(0, mate_0)
    second_0 = lax.ppermute(held_0, "section", to_lower)

    far_1, _ = lax.optimization_barrier((owns[1][2], held_0))
    mates.append(lax.ppermute(far_1, "section", to_mate))

    second_0, _ = lax.optimization_barrier((second_0, own))
    passed_0 = forward(0, second_0, mate_0, held_0)
    third_0 = lax.ppermute(passed_0, "section", to_other)

    mate_1, _ = lax.optimization_barrier((mates[1], passed_0))
    held_1 = hold(1, mate_1)
    second_1 = lax.ppermute(held_1, "section", to_lower)

    block, _ = lax.optimization_barrier((block, held_1))
    sent = solve(y_index, stats, block)

    second_1, _ = lax.optimization_barrier((second_1, sent))
    passed_1 = forward(1, second_1, mate_1, held_1)
    third_1 = lax.ppermute(passed_1, "section", to_other)
    nears = [
        finished(0, second_0, mate_0, held_0, passed_1),
        finished(1, second_1, mate_1, held_1, passed_1),
    ]
    thirds, _ = lax.optimization_barrier(([third_0, third_1], nears))
    fars = [(third, owns[k][1], top_far[k]) for k, third in enumerate(thirds)]
    back = exchange(sent, X_GROUPS)
    weight_grad, new_left, new_right, roots = finish(
        refresh[0, 0], back, left_stats[0], right_stats[0]
    )
    fars = [
        jnp.where(
            section == 2,
            third,
            (jnp.where(section == 3, above, third).astype(f32) + far).astype(bf16),
        )
        for third, far, above in fars
    ]
    near, far = jnp.concatenate(nears, axis=1), jnp.concatenate(fars, axis=1)
    section_grad = jnp.concatenate(
        [jnp.where(is_left, near, far), jnp.where(is_left, far, near)], axis=1
    ).reshape(micro, tok_dev, width)
    return (
        section_grad[None],
        weight_grad[None],
        new_left[None],
        new_right[None],
        roots[None, None],
    )


def solution(mesh):
    return jax.shard_map(
        per_device,
        mesh=mesh,
        in_specs=(
            P(None, "dp", "tensor"),
            P("section", None, "dp", "tensor"),
            P("section", None, "dp", "tensor"),
            P("section", "dp", "tensor"),
            P("section", "tensor", "dp", None),
            P("section", "tensor", "dp", None),
            P("section", "tensor", None),
            P(),
        ),
        out_specs=(
            P("section", None, "dp", "tensor"),
            P("section", "dp", "tensor"),
            P("section", "tensor", "dp", None),
            P("section", "tensor", "dp", None),
            P("section", "tensor", None, "dp", None),
        ),
        check_vma=False,
    )
```

```python
import jax
import jax.numpy as jnp
from jax import lax
from jax.experimental import pallas as pl
from jax.experimental.pallas import tpu as pltpu
from jax.sharding import PartitionSpec as P

EPS = 1e-06

NX = 4
NY = 8
X_GROUPS = [[x * NY + y for x in range(NX)] for y in range(NY)]
Y_GROUPS = [[x * NY + y for y in range(NY)] for x in range(NX)]
PIECE = 256
SPLIT = 3
PARAMS = pltpu.CompilerParams(vmem_limit_bytes=40 * 1024 * 1024)
WIDE = pltpu.CompilerParams(vmem_limit_bytes=56 * 1024 * 1024)


def exchange(block, groups):
    return lax.all_to_all(block, "dp", 0, 0, axis_index_groups=groups, tiled=True)


def pack_kernel(weight, left, right, packed):
    own = weight.shape[0]
    per_half = weight.shape[1] // (2 * PIECE)
    rest = per_half - SPLIT

    def put(x, group, piece):
        packed[x, group * own : (group + 1) * own, :] = piece

    group = 0
    for ref in (left, right):
        for p in range(ref.shape[2] // PIECE):
            for x in range(NX):
                put(x, group, ref[x, :, p * PIECE : (p + 1) * PIECE].astype(jnp.bfloat16))
            group += 1
    for h in range(2):
        for p in range(per_half):
            place = h * SPLIT + p if p < SPLIT else 2 * SPLIT + h * rest + p - SPLIT
            column = (h * per_half + p) * PIECE
            for x in range(NX):
                put(x, group + place, weight[:, column : column + PIECE])


def pack(weight, left, right):
    own, width = weight.shape
    rows = own * (width + 2 * left.shape[2]) // PIECE
    return pl.pallas_call(
        pack_kernel,
        grid=(1,),
        in_specs=[
            pl.BlockSpec(weight.shape, lambda i: (0, 0)),
            pl.BlockSpec(left.shape, lambda i: (0, 0, 0)),
            pl.BlockSpec(right.shape, lambda i: (0, 0, 0)),
        ],
        out_specs=pl.BlockSpec((NX, rows, PIECE), lambda i: (0, 0, 0)),
        out_shape=jax.ShapeDtypeStruct((NX, rows, PIECE), jnp.bfloat16),
        cost_estimate=pl.CostEstimate(
            flops=1024, bytes_accessed=1024 * 1024, transcendentals=0
        ),
        compiler_params=WIDE,
    )(weight, left, right)


def partial_kernel(order, values, inputs, result):
    total = 0.0
    for k in range(inputs.shape[0]):
        total += lax.dot_general(
            values[order[k]],
            inputs[k],
            (((0,), (0,)), ((), ())),
            preferred_element_type=jnp.float32,
        )
    result[0] = total.astype(jnp.bfloat16)


def partial_gradient(order, values, inputs):
    micro, tokens, kv = values.shape
    blocks = inputs.shape[2] // kv
    return pl.pallas_call(
        partial_kernel,
        grid_spec=pltpu.PrefetchScalarGridSpec(
            num_scalar_prefetch=1,
            grid=(blocks,),
            in_specs=[
                pl.BlockSpec((micro, tokens, kv), lambda b, o: (0, 0, 0)),
                pl.BlockSpec((micro, tokens, kv), lambda b, o: (0, 0, b)),
            ],
            out_specs=pl.BlockSpec((1, kv, kv), lambda b, o: (b, 0, 0)),
        ),
        out_shape=jax.ShapeDtypeStruct((blocks, kv, kv), jnp.bfloat16),
        cost_estimate=pl.CostEstimate(
            flops=2 * micro * tokens * kv * kv * blocks,
            bytes_accessed=3 * 1024 * 1024,
            transcendentals=0,
        ),
        compiler_params=PARAMS,
    )(order, values, inputs)


def over_x_kernel(parts, result):
    own = result.shape[2]
    for x in range(NX):
        for y in range(NY):
            place = slice((x * NY + y) * own, (x * NY + y + 1) * own)
            total = parts[0, place, :].astype(jnp.float32)
            for k in range(1, NX):
                total += parts[k, place, :].astype(jnp.float32)
            result[y, x] = total.astype(jnp.bfloat16)


def over_y_kernel(parts, result):
    total = parts[0].astype(jnp.float32)
    for k in range(1, NY):
        total += parts[k].astype(jnp.float32)
    total = total.astype(jnp.bfloat16)
    for k in range(NY):
        result[k] = total


def whole_call(kernel, out_shape, *operands):
    vmem = pl.BlockSpec(memory_space=pltpu.VMEM)
    return pl.pallas_call(
        kernel,
        in_specs=[vmem] * len(operands),
        out_specs=vmem,
        out_shape=out_shape,
        cost_estimate=pl.CostEstimate(
            flops=1024, bytes_accessed=2 * 1024 * 1024, transcendentals=0
        ),
        compiler_params=PARAMS,
    )(*operands)


def own_kernel(half, values, *refs):
    rows = values.shape[1]
    count = (len(refs) - 3) // 2
    near, far, far_sent = refs[2 * count :]
    for p in range(count):
        place = slice(p * PIECE, (p + 1) * PIECE)
        of_near, of_far = [
            jnp.dot(values[...], weight[...].reshape(rows, PIECE), preferred_element_type=jnp.float32)
            for weight in (refs[p], refs[count + p])
        ]
        near[:, place] = of_near
        far[:, place] = of_far
        far_sent[:, place] = of_far.astype(jnp.bfloat16)


def own_contribution(half, values, pieces):
    tokens, kv = values.shape
    shape = (NY, NX, kv // (NX * NY), PIECE)
    width = len(pieces) * PIECE
    result = pl.BlockSpec((tokens, width), lambda i, h: (0, 0))

    def near(first, stride):
        return pl.BlockSpec(shape, lambda i, h: (0, 0, first + h[0] * stride, 0))

    def far(first, stride):
        return pl.BlockSpec(shape, lambda i, h: (0, 0, first + (1 - h[0]) * stride, 0))

    arrays = [array for array, _, _ in pieces]
    return pl.pallas_call(
        own_kernel,
        grid_spec=pltpu.PrefetchScalarGridSpec(
            num_scalar_prefetch=1,
            grid=(1,),
            in_specs=[pl.BlockSpec((tokens, kv), lambda i, h: (0, 0))]
            + [near(first, stride) for _, first, stride in pieces]
            + [far(first, stride) for _, first, stride in pieces],
            out_specs=[result, result, result],
        ),
        out_shape=[
            jax.ShapeDtypeStruct((tokens, width), jnp.float32),
            jax.ShapeDtypeStruct((tokens, width), jnp.float32),
            jax.ShapeDtypeStruct((tokens, width), jnp.bfloat16),
        ],
        cost_estimate=pl.CostEstimate(
            flops=4 * tokens * kv * width,
            bytes_accessed=len(pieces) * 1536 * 1024,
            transcendentals=0,
        ),
        compiler_params=PARAMS,
    )(half.reshape(1).astype(jnp.int32), values, *arrays, *arrays)


def solve_kernel(y_ref, stats, block, sent, rows, left, right, matrix):
    own, size = block.shape[2:]
    y = y_ref[0]
    for x in range(NX):
        for other in range(NY):
            place = slice((x * NY + other) * own, (x * NY + other + 1) * own)
            rows[place, :] = block[other, x]
            for side, ref in enumerate((left, right)):
                for p in range(size // PIECE):
                    group = side * (size // PIECE) + p
                    ref[place, p * PIECE : (p + 1) * PIECE] = stats[
                        other, x, group * own : (group + 1) * own, :
                    ].astype(jnp.float32)
    whole = rows[...]
    starts = [pl.multiple_of(x * NY * own + y * own, own) for x in range(NX)]

    def mine(ref):
        return jnp.concatenate([ref[pl.ds(start, own), :] for start in starts], axis=0)

    picked = mine(rows)
    for x in range(NX):
        sent[x, 0] = picked[x * own : (x + 1) * own]
    line = lax.broadcasted_iota(jnp.int32, (NX * own, size), 0)
    line = (line // own) * (NY * own) + y * own + line % own
    column = lax.broadcasted_iota(jnp.int32, (NX * own, size), 1)
    identity = jnp.where(line == column, 1.0, 0.0)
    for side, (ref, dims) in enumerate(((left, 1), (right, 0))):
        gram = lax.dot_general(
            whole, whole, (((dims,), (dims,)), ((), ())), preferred_element_type=jnp.float32
        )
        stat = ref[...] + gram
        ref[...] = stat
        now = mine(ref)
        total = jnp.sum(stat * stat, axis=1, keepdims=True)
        total = jnp.sum(total, axis=0, keepdims=True) / (size * size)
        scale = 1.0 / (jnp.sqrt(total + EPS) * size)
        matrix[...] = (stat * scale).astype(jnp.bfloat16)
        first = now * scale
        term = first
        for _ in range(5):
            term = 1.25 * term - 0.25 * jnp.dot(
                term.astype(jnp.bfloat16), matrix[...], preferred_element_type=jnp.float32
            )
        root = 0.25 * (6.25 * identity - 1.25 * first - term)
        root = root.astype(jnp.bfloat16)
        ref[...] = gram
        gram_rows = mine(ref).astype(jnp.bfloat16)
        for x in range(NX):
            part = slice(x * own, (x + 1) * own)
            sent[x, 1 + side] = gram_rows[part]
            sent[x, 3 + side] = root[part]


def solve(y_index, gathered, block):
    own, size = block.shape[2:]
    vmem = pl.BlockSpec(memory_space=pltpu.VMEM)
    return pl.pallas_call(
        solve_kernel,
        in_specs=[pl.BlockSpec(memory_space=pltpu.SMEM), vmem, vmem],
        out_specs=vmem,
        out_shape=jax.ShapeDtypeStruct((NX, 5, own, size), jnp.bfloat16),
        scratch_shapes=[
            pltpu.VMEM((size, size), jnp.bfloat16),
            pltpu.VMEM((size, size), jnp.float32),
            pltpu.VMEM((size, size), jnp.float32),
            pltpu.VMEM((size, size), jnp.bfloat16),
        ],
        cost_estimate=pl.CostEstimate(
            flops=3 * 2 * size**3, bytes_accessed=2 * 1024 * 1024, transcendentals=0
        ),
        compiler_params=PARAMS,
    )(y_index.reshape(1).astype(jnp.int32), gathered, block)


def finish_kernel(refresh, back, left_stats, right_stats, weight_grad, new_left, new_right, roots):
    size = back.shape[-1]
    for b in range(NX):
        weight_grad[:, b * size : (b + 1) * size] = back[b, 0].astype(jnp.float32)
        new_left[b] = left_stats[b] + back[b, 1].astype(jnp.float32)
        new_right[b] = right_stats[b] + back[b, 2].astype(jnp.float32)
    for k in range(roots.shape[0] // 2):
        chosen = refresh[k]
        roots[2 * k] = back[chosen, 3].astype(jnp.float32)
        roots[2 * k + 1] = back[chosen, 4].astype(jnp.float32)


def finish(refresh, back, left_stats, right_stats):
    own, size = back.shape[2:]
    picks = 2 * refresh.shape[0]
    shapes = [
        (own, NX * size),
        left_stats.shape,
        right_stats.shape,
        (picks, own, size),
    ]
    vmem = pl.BlockSpec(memory_space=pltpu.VMEM)
    return pl.pallas_call(
        finish_kernel,
        in_specs=[pl.BlockSpec(memory_space=pltpu.SMEM), vmem, vmem, vmem],
        out_specs=[vmem] * 4,
        out_shape=[jax.ShapeDtypeStruct(s, jnp.float32) for s in shapes],
        cost_estimate=pl.CostEstimate(
            flops=1024, bytes_accessed=2 * 1024 * 1024, transcendentals=0
        ),
        compiler_params=PARAMS,
    )(refresh, back, left_stats, right_stats)


def per_device(top_grad, stash, value_grad, value_weight, left_stats, right_stats, refresh, order):
    micro, tok_dev, width = top_grad.shape
    rows_own = value_weight.shape[1]
    kv = left_stats.shape[3]
    tokens = micro * tok_dev
    section = lax.axis_index("section")
    y_index = lax.axis_index("dp") % NY

    value_full = lax.all_gather(value_grad[0], "tensor", axis=2, tiled=True)

    per_half = width // (2 * PIECE)
    groups = 2 * kv // PIECE
    early = (groups + 2 * SPLIT) * rows_own
    first = exchange(pack(value_weight[0], left_stats[0], right_stats[0]), X_GROUPS)
    first, value_full = lax.optimization_barrier((first, value_full))
    late = groups * rows_own
    gathered = lax.all_gather(first[:, late:early], "dp", axis=0, axis_index_groups=Y_GROUPS)
    stats, _ = lax.optimization_barrier((first[:, :late], gathered))
    stats = lax.all_gather(stats, "dp", axis=0, axis_index_groups=Y_GROUPS)

    partial = partial_gradient(order, value_full, stash[0])
    over_x = exchange(partial, X_GROUPS)
    last, _ = lax.optimization_barrier((first[:, early:], partial))
    last = lax.all_gather(last, "dp", axis=0, axis_index_groups=Y_GROUPS)

    value_own = value_full.reshape(tokens, NX, NY, rows_own).transpose(0, 2, 1, 3)
    value_own = value_own.reshape(tokens, kv)
    is_left = (section == 1) | (section == 2)
    half = jnp.where(is_left, 0, 1)
    pieces = [(gathered, p, SPLIT) for p in range(SPLIT)] + [(last, 0, 1)]
    owns = [own_contribution(half, value_own, part) for part in (pieces[:2], pieces[2:])]
    to_mate = [(3, 2), (2, 3), (1, 0)]
    mates = [lax.ppermute(owns[0][2], "section", to_mate)]

    top = top_grad.reshape(tokens, width)
    cols = 2 * PIECE
    left_top, right_top = [
        [top[:, start + k * cols : start + (k + 1) * cols] for k in range(2)]
        for start in (0, width // 2)
    ]
    top_near = [jnp.where(is_left, a, b) for a, b in zip(left_top, right_top)]
    top_far = [jnp.where(is_left, b, a) for a, b in zip(left_top, right_top)]
    over_x, _ = lax.optimization_barrier((over_x, (last, top_near, top_far, value_own)))
    split_shape = jax.ShapeDtypeStruct((NY, NX, rows_own, kv), jnp.bfloat16)
    by_y = whole_call(over_x_kernel, split_shape, over_x)
    over_y = exchange(by_y, Y_GROUPS)

    f32, bf16 = jnp.float32, jnp.bfloat16

    def hold(k, mate):
        return (top_near[k].astype(f32) + (owns[k][0] + mate.astype(f32))).astype(bf16)

    def update(second, near, mate):
        return (second.astype(f32) + (near + mate.astype(f32))).astype(bf16)

    def forward(k, second, mate, held):
        updated = update(second, owns[k][0], mate)
        return jnp.where(section == 0, second, jnp.where(section == 1, updated, held))

    def finished(k, second, mate, held, after):
        second, mate, near, _ = lax.optimization_barrier((second, mate, owns[k][0], after))
        alone = (top_near[k].astype(f32) + near).astype(bf16)
        updated = update(second, near, mate)
        return jnp.where(section == 3, alone, jnp.where(section == 2, held, updated))

    to_lower = [(2, 1), (3, 0)]
    to_other = [(1, 0), (0, 1), (3, 2)]
    over_y, _ = lax.optimization_barrier((over_y, owns))
    own = whole_call(over_y_kernel, split_shape, over_y)
    block = exchange(own, Y_GROUPS)

    mate_0, _ = lax.optimization_barrier((mates[0], own))
    held_0 = hold(0, mate_0)
    second_0 = lax.ppermute(held_0, "section", to_lower)

    far_1, _ = lax.optimization_barrier((owns[1][2], held_0))
    mates.append(lax.ppermute(far_1, "section", to_mate))

    second_0, _ = lax.optimization_barrier((second_0, own))
    passed_0 = forward(0, second_0, mate_0, held_0)
    third_0 = lax.ppermute(passed_0, "section", to_other)

    mate_1, _ = lax.optimization_barrier((mates[1], passed_0))
    held_1 = hold(1, mate_1)
    second_1 = lax.ppermute(held_1, "section", to_lower)

    block, _ = lax.optimization_barrier((block, held_1))
    sent = solve(y_index, stats, block)

    second_1, _ = lax.optimization_barrier((second_1, sent))
    passed_1 = forward(1, second_1, mate_1, held_1)
    third_1 = lax.ppermute(passed_1, "section", to_other)
    nears = [
        finished(0, second_0, mate_0, held_0, passed_1),
        finished(1, second_1, mate_1, held_1, passed_1),
    ]
    thirds, _ = lax.optimization_barrier(([third_0, third_1], nears))
    fars = [(third, owns[k][1], top_far[k]) for k, third in enumerate(thirds)]
    back = exchange(sent, X_GROUPS)
    weight_grad, new_left, new_right, roots = finish(
        refresh[0, 0], back, left_stats[0], right_stats[0]
    )
    fars = [
        jnp.where(
            section == 2,
            third,
            (jnp.where(section == 3, above, third).astype(f32) + far).astype(bf16),
        )
        for third, far, above in fars
    ]
    near, far = jnp.concatenate(nears, axis=1), jnp.concatenate(fars, axis=1)
    section_grad = jnp.concatenate(
        [jnp.where(is_left, near, far), jnp.where(is_left, far, near)], axis=1
    ).reshape(micro, tok_dev, width)
    return (
        section_grad[None],
        weight_grad[None],
        new_left[None],
        new_right[None],
        roots[None, None],
    )


def solution(mesh):
    return jax.shard_map(
        per_device,
        mesh=mesh,
        in_specs=(
            P(None, "dp", "tensor"),
            P("section", None, "dp", "tensor"),
            P("section", None, "dp", "tensor"),
            P("section", "dp", "tensor"),
            P("section", "tensor", "dp", None),
            P("section", "tensor", "dp", None),
            P("section", "tensor", None),
            P(),
        ),
        out_specs=(
            P("section", None, "dp", "tensor"),
            P("section", "dp", "tensor"),
            P("section", "tensor", "dp", None),
            P("section", "tensor", "dp", None),
            P("section", "tensor", None, "dp", None),
        ),
        check_vma=False,
    )
```
